32 devices in a mesh: pair: 2 (over x), row: 4 (over y, core), col: 4 (over z).
Axes of the slice: x: 2, y: 2, z: 4, core: 2. Of those that a mesh axis runs over, the one named last changes fastest.
Arguments:
- features: bfloat16 [2, 64, 64, 512], P('pair', None, 'row', 'col'), may hold values from -6 to 6
- offsets: int32 [2, 2, 64, 512], P('pair', None, 'row', 'col'), may hold values from -8 to 7
- fractions: int32 [2, 2, 64, 512], P('pair', None, 'row', 'col'), may hold values from 0 to 255
- tissue: int32 [2, 8, 64], P('pair', 'row', 'col'), may hold values 0 or 1
- w_first: bfloat16 [9, 64, 128], replicated, may hold values from -0.1875 to 0.1875
- w_second: bfloat16 [9, 64, 64], replicated, may hold values from -0.25 to 0.25
- head_weight: bfloat16 [2, 64], replicated, may hold values from -0.75 to 0.75
Outputs:
- warped_features: bfloat16 [2, 64, 64, 512], P('pair', None, 'row', 'col')
- motion_field: float32 [2, 2, 64, 512], P('pair', None, 'row', 'col')
The draws below stay inside these ranges and needn't reach their ends.
All inputs are finite; a program needn't handle non-finite values. No bound on the sum of `tissue` on one device may be relied on, other than what follows from the above.
Results may differ from the reference program's by a relative error of at most 0.0056.
Values may be sent and summed in bfloat16 or wider, within the bound.
A program may use at most 64 MiB of HBM per device.

```python
import jax
import jax.numpy as jnp
from jax import lax

C = 64
MAXS = 8
BLK = 8
NR = 64
NC = 512


def draw_offsets(key, part):
    values = jax.random.randint(key, (2, 2, NR, NC), -MAXS, MAXS, dtype=jnp.int32)
    values = values.at[0, 0, 0, 0].set(-MAXS)
    values = values.at[1, 1, NR - 1, NC - 1].set(MAXS - 1)
    return values


def plant(result, own_key, smallest, high):
    longest = result.shape.index(max(result.shape))
    spots = []
    for shift in (0, 1):
        where = [jax.random.randint(jax.random.fold_in(own_key, axis), (), 0, length) for axis, length in enumerate(result.shape)]
        where[longest] = (where[longest] + shift) % result.shape[longest]
        spots.append(tuple(where))
    return result.at[spots[0]].set(smallest).at[spots[1]].set(high)


def block_levels(rng, dims, shards, smallest, largest):
    def one(dim, shards_of):
        steps = jax.random.uniform(jax.random.fold_in(jax.random.fold_in(rng, 6), dim), (shards_of,), jnp.float32, smallest / len(shards), largest / len(shards))
        return jnp.repeat(jnp.exp(steps), dims[dim] // shards_of).reshape((-1,) + (1,) * (len(dims) - dim - 1))

    gain = one(*shards[0])
    for cut in shards[1:]:
        gain = gain * one(*cut)
    return gain


def centred(own_key, shape, deviation, most, cuts=(), held_as=jnp.bfloat16):
    gain = block_levels(own_key, shape, cuts, -0.22, 0.18) if cuts else 1.0
    values = jax.random.normal(own_key, shape, jnp.float32) * deviation * gain
    return jnp.minimum(jnp.maximum(values, -most), most).astype(held_as)


def setup_inputs(seed: int = 0) -> dict:
    key_list = jax.random.split(jax.random.key(seed), 8)
    return {
        "features": centred(key_list[0], (2, C, NR, NC), 1.0, 6.0, ((0, 2), (2, 4), (3, 4))),
        "offsets": draw_offsets(jax.random.fold_in(key_list[7], 71), 0),
        "fractions": plant(jax.random.randint(key_list[2], (2, 2, NR, NC), 0, 256), jax.random.fold_in(key_list[2], 1), 0, 255).astype(jnp.int32),
        "tissue": plant((jax.random.randint(key_list[3], (2, NR // BLK, NC // BLK), 0, 4) < 3).astype(jnp.int32), jax.random.fold_in(key_list[3], 1), 0, 1),
        "w_first": centred(key_list[4], (9, C, 2 * C), (18 * C) ** -0.5, 0.1875),
        "w_second": centred(key_list[5], (9, C, C), (9 * C) ** -0.5, 0.25),
        "head_weight": centred(key_list[6], (2, C), C ** -0.5, 0.75),
    }


frac_scale = 256.0


def convolve(padded, weights, height, columns):
    summed = None
    for tap_index in range(9):
        row_shift = tap_index // 3
        col_shift = tap_index % 3
        window = padded[:, row_shift:row_shift + height, col_shift:col_shift + columns]
        window = window.reshape(padded.shape[0], height * columns)
        product = jnp.dot(weights[tap_index], window, preferred_element_type=jnp.float32)
        summed = product if summed is None else summed + product
    return summed.reshape(weights.shape[1], height, columns)


def sample(source, motion, margin, height, columns):
    stride = columns + 2 * margin
    grid_rows = lax.broadcasted_iota(jnp.int32, (height, columns), 0).astype(jnp.float32)
    grid_cols = lax.broadcasted_iota(jnp.int32, (height, columns), 1).astype(jnp.float32)
    place_row = grid_rows + motion[0] + margin
    place_col = grid_cols + motion[1] + margin
    floor_row = jnp.floor(place_row)
    floor_col = jnp.floor(place_col)
    frac_row = place_row - floor_row
    frac_col = place_col - floor_col
    base_index = floor_row.astype(jnp.int32) * stride + floor_col.astype(jnp.int32)
    flat_source = source.reshape(source.shape[0], -1)

    def fetch(step_size):
        picked = jnp.take(flat_source, (base_index + step_size).reshape(-1), axis=1, mode="clip")
        return picked.reshape(source.shape[0], height, columns).astype(jnp.float32)

    blended = (1.0 - frac_row) * (1.0 - frac_col) * fetch(0) + (1.0 - frac_row) * frac_col * fetch(1)
    blended = blended + frac_row * (1.0 - frac_col) * fetch(stride)
    blended = blended + frac_row * frac_col * fetch(stride + 1)
    return blended.astype(jnp.bfloat16)


def reference(features, offsets, fractions, tissue, w_first, w_second, head_weight):
    margin = MAXS + 1
    warped_list = []
    motion_list = []
    for section in range(2):
        own_features = features[section]
        partner = features[1 - section]
        joined = jnp.concatenate([own_features, partner], axis=0)
        padded_joined = jnp.pad(joined, ((0, 0), (1, 1), (1, 1)))
        hidden_one = jax.nn.relu(convolve(padded_joined, w_first, NR, NC)).astype(jnp.bfloat16)
        padded_hidden = jnp.pad(hidden_one, ((0, 0), (1, 1), (1, 1)))
        hidden_two = jax.nn.relu(convolve(padded_hidden, w_second, NR, NC)).astype(jnp.bfloat16)
        residual = jnp.tanh(jnp.dot(head_weight, hidden_two.reshape(C, NR * NC), preferred_element_type=jnp.float32))
        residual = residual.reshape(2, NR, NC)
        coverage = jnp.repeat(jnp.repeat(tissue[section], BLK, axis=0), BLK, axis=1).astype(jnp.float32)
        motion = offsets[section].astype(jnp.float32) + fractions[section].astype(jnp.float32) / frac_scale
        motion = motion + coverage[None] * residual
        banded = jnp.pad(own_features, ((0, 0), (margin, margin), (margin, margin)))
        warped_list.append(sample(banded, motion, margin, NR, NC))
        motion_list.append(motion)
    return jnp.stack(warped_list), jnp.stack(motion_list)
```

```python
import functools

import jax
import jax.numpy as jnp
from jax import lax
from jax.experimental import pallas as pl
from jax.experimental.pallas import tpu as pltpu
from jax.sharding import PartitionSpec as P

MAXS = 8
BLK = 8
MARGIN = MAXS + 1
FRAC_SCALE = 256.0
STRIP = 16
MESH = pl.DeviceIdType.MESH

STRIPS = [(dr, dc) for dr in (-1, 0, 1) for dc in (-1, 1)]
N_COPIES = 12


def lanes(shape):
    return lax.broadcasted_iota(jnp.int32, shape, len(shape) - 1)


def kernel(
    n_row,
    n_col,
    feat,
    offsets,
    fractions,
    tissue,
    w_first,
    w_second,
    head,
    out,
    motion_out,
    own,
    other,
    packed,
    strips,
    package,
    hidden,
    hidden_two,
    send_sem,
    recv_sem,
):
    height, channels, columns = feat.shape
    slots = columns // STRIP
    pair = lax.axis_index("pair")
    row = lax.axis_index("row")
    col = lax.axis_index("col")

    def exists(dr, dc):
        ok = None
        for test in (
            [row + dr >= 0, row + dr < n_row] if dr else []
        ) + ([col + dc >= 0, col + dc < n_col] if dc else []):
            ok = test if ok is None else jnp.logical_and(ok, test)
        return ok

    neighbours = [(dr, dc) for dr in (-1, 0, 1) for dc in (-1, 0, 1) if dr or dc]
    barrier = pltpu.get_barrier_semaphore()
    pl.semaphore_signal(
        barrier, inc=1, device_id=(1 - pair, row, col), device_id_type=MESH
    )
    expected = jnp.int32(1)
    for dr, dc in neighbours:
        here = exists(dr, dc)
        expected = expected + here.astype(jnp.int32)

        @pl.when(here)
        def _():
            pl.semaphore_signal(
                barrier, inc=1, device_id=(pair, row + dr, col + dc), device_id_type=MESH
            )

    lane = lanes((channels, columns))
    slot = lane // STRIP
    for plane in range(height // slots):
        first = jnp.zeros((channels, columns), jnp.float32)
        last = first
        for k in range(slots):
            value = feat[plane * slots + k].astype(jnp.float32)
            if k:
                value = pltpu.roll(value, STRIP * k, 1)
            first = jnp.where(slot == k, value, first)
            last = jnp.where(slot == (k - 1) % slots, value, last)
        packed[0, plane] = first.astype(jnp.bfloat16)
        packed[1, plane] = last.astype(jnp.bfloat16)

    pl.semaphore_wait(barrier, expected)

    def copy(index, source, target, device):
        return pltpu.make_async_remote_copy(
            src_ref=source,
            dst_ref=target,
            send_sem=send_sem.at[index],
            recv_sem=recv_sem.at[index],
            device_id=device,
            device_id_type=MESH,
        )

    partner = (1 - pair, row, col)
    low = pl.ds(0, columns)
    to_partner = copy(0, feat, other.at[pl.ds(2, height), :, low], partner)
    near = []
    for n, (dr, dc) in enumerate(STRIPS):
        near.append(
            (
                copy(
                    3 + n,
                    packed.at[0 if dc < 0 else 1],
                    strips.at[n],
                    (pair, row + dr, col + dc),
                ),
                (dr, dc),
                strips.at[n],
            )
        )
    for index, dr, source, target in (
        (1, 1, pl.ds(height - MARGIN, MARGIN), pl.ds(0, MARGIN)),
        (2, -1, pl.ds(0, MARGIN), pl.ds(height + MARGIN, MARGIN)),
    ):
        place = own.at[target, :, low]
        near.append((copy(index, feat.at[source], place, (pair, row + dr, col)), (dr, 0), place))

    for moved, (dr, dc), _ in near:
        pl.when(exists(dr, dc))(moved.start)
    to_partner.start()
    for _, (dr, dc), place in near:

        @pl.when(jnp.logical_not(exists(-dr, -dc)))
        def _():
            place[...] = jnp.zeros(place.shape, place.dtype)

    own[pl.ds(MARGIN, height), :, low] = feat[...]

    w_one = jnp.concatenate([w_first[pl.ds(192 * a, 192), :] for a in range(3)], axis=1)
    w_two = jnp.concatenate([w_second[pl.ds(192 * a, 192), :] for a in range(3)], axis=1)

    for moved, (dr, dc), _ in near:
        pl.when(exists(-dr, -dc))(moved.wait_recv)

    bundle = jnp.zeros((channels, columns), jnp.float32)
    for i in range(height + 2 * MARGIN):
        side = -1 if i < MARGIN else (0 if i < MARGIN + height else 1)
        k = i - MARGIN - side * height
        left = strips[STRIPS.index((-side, 1)), k // slots].astype(jnp.float32)
        right = strips[STRIPS.index((-side, -1)), k // slots].astype(jnp.float32)
        k = k % slots
        value = jnp.where(
            slot == k, right, jnp.where(slot == (k - 1) % slots, left, 0.0)
        )
        if k:
            value = pltpu.roll(value, columns - STRIP * k, 1)
        own[i, :, pl.ds(columns, columns)] = value.astype(jnp.bfloat16)
        j = i - MARGIN + 2
        if 0 <= j < height + 4:
            bundle = jnp.where(lane // 4 == j, pltpu.roll(value, 2 + 4 * j, 1), bundle)
    package[0] = bundle.astype(jnp.bfloat16)

    passed = [
        copy(9, package.at[0], package.at[1], partner),
        copy(
            10,
            own.at[pl.ds(MARGIN - 2, 2), :, low],
            other.at[pl.ds(0, 2), :, low],
            partner,
        ),
        copy(
            11,
            own.at[pl.ds(MARGIN + height, 2), :, low],
            other.at[pl.ds(height + 2, 2), :, low],
            partner,
        ),
    ]
    for moved in passed:
        moved.start()
    to_partner.wait_recv()
    for moved in passed:
        moved.wait_recv()
    bundle = package[1].astype(jnp.float32)
    for j in range(height + 4):
        other[j, :, pl.ds(columns, columns)] = pltpu.roll(
            bundle, (2 * columns - 2 - 4 * j) % columns, 1
        ).astype(jnp.bfloat16)

    wide = 2 * columns

    def joined_taps(z):
        return (
            pltpu.roll(z[:channels], 1, 1)
            + z[channels : 2 * channels]
            + pltpu.roll(z[2 * channels :], wide - 1, 1)
        )

    wide_lane = lanes((channels, wide))
    place_col = jnp.where(wide_lane < wide * 3 // 4, wide_lane, wide_lane - wide) + col * columns
    col_ok = jnp.logical_and(place_col >= 0, place_col < n_col * columns)

    def first_layer(step, carry):
        for part in range(3):
            y = step * 3 + part
            window = jnp.concatenate(
                [
                    piece
                    for a in range(3)
                    for piece in (own[y + MARGIN - 2 + a], other[y + a])
                ],
                axis=0,
            )
            value = joined_taps(jnp.dot(w_one, window, preferred_element_type=jnp.float32))
            place_row = row * height + y - 1
            row_ok = jnp.logical_and(place_row >= 0, place_row < n_row * height)
            ok = jnp.logical_and(col_ok, row_ok)
            hidden[y] = jnp.where(ok, jnp.maximum(value, 0.0), 0.0).astype(jnp.bfloat16)
        return carry

    lax.fori_loop(0, (height + 2) // 3, first_layer, 0)

    for y in range(height):
        window = jnp.concatenate([hidden[y + a] for a in range(3)], axis=0)
        value = joined_taps(jnp.dot(w_two, window, preferred_element_type=jnp.float32))
        hidden_two[:, pl.ds(y * columns, columns)] = jnp.maximum(value[:, :columns], 0.0).astype(
            jnp.bfloat16
        )

    residual = jnp.tanh(
        jnp.dot(head[...], hidden_two[...], preferred_element_type=jnp.float32)
    )
    cells = columns // BLK
    spread = (
        lax.broadcasted_iota(jnp.int32, (cells, columns), 1) // BLK
        == lax.broadcasted_iota(jnp.int32, (cells, columns), 0)
    ).astype(jnp.bfloat16)
    coverage = jnp.dot(
        tissue[...].astype(jnp.float32).astype(jnp.bfloat16),
        spread,
        preferred_element_type=jnp.float32,
    )
    for y in range(height):
        cover = coverage[y // BLK : y // BLK + 1]
        for k in range(2):
            motion_out[k, pl.ds(y, 1), :] = (
                offsets[k, pl.ds(y, 1), :].astype(jnp.float32)
                + fractions[k, pl.ds(y, 1), :].astype(jnp.float32) / FRAC_SCALE
                + cover * residual[k : k + 1, y * columns : (y + 1) * columns]
            )

    depth = 2 * MARGIN + 2
    source = lax.broadcasted_iota(jnp.int32, (wide, wide), 0)
    source = jnp.where(source < wide * 3 // 4, source, source - wide).astype(jnp.float32)
    target = lanes((1, wide))
    target_col = (target % columns).astype(jnp.float32)
    target_row = (target // columns).astype(jnp.float32)
    reach = lax.broadcasted_iota(jnp.int32, (depth, wide), 0).astype(jnp.float32) - MARGIN

    def warp(t, carry):
        y = 2 * t
        both = [
            jnp.concatenate(
                [motion_out[k, pl.ds(y, 1), :], motion_out[k, pl.ds(y + 1, 1), :]], axis=1
            )
            for k in range(2)
        ]
        col_weight = jnp.maximum(1.0 - jnp.abs(both[1] + target_col - source), 0.0)
        row_weight = jnp.maximum(1.0 - jnp.abs(both[0] + target_row - reach), 0.0)
        rows = own[pl.ds(y, depth)].reshape(depth * channels, wide)
        picked = jnp.dot(
            rows, col_weight.astype(jnp.bfloat16), preferred_element_type=jnp.float32
        )
        total = None
        for d in range(depth):
            term = picked[d * channels : (d + 1) * channels] * row_weight[d : d + 1]
            total = term if total is None else total + term
        total = total.astype(jnp.bfloat16)
        out[y] = total[:, :columns]
        out[y + 1] = total[:, columns:]
        return carry

    lax.fori_loop(0, height // 2, warp, 0)

    for moved, (dr, dc), _ in near:
        pl.when(exists(dr, dc))(moved.wait_send)
    to_partner.wait_send()
    for moved in passed:
        moved.wait_send()


def shards(n_row, n_col, features, offsets, fractions, tissue, w_first, w_second, head_weight):
    _, channels, height, columns = features.shape
    feat = jnp.transpose(features[0], (1, 0, 2))
    wide = 2 * columns
    vmem = pl.BlockSpec(memory_space=pltpu.VMEM)
    warped, motion = pl.pallas_call(
        functools.partial(kernel, n_row, n_col),
        out_shape=(
            jax.ShapeDtypeStruct((height, channels, columns), jnp.bfloat16),
            jax.ShapeDtypeStruct((2, height, columns), jnp.float32),
        ),
        in_specs=[vmem] * 7,
        out_specs=(vmem, vmem),
        scratch_shapes=[
            pltpu.VMEM((height + 2 * MARGIN, channels, wide), jnp.bfloat16),
            pltpu.VMEM((height + 4, channels, wide), jnp.bfloat16),
            pltpu.VMEM((2, 2, channels, columns), jnp.bfloat16),
            pltpu.VMEM((6, 2, channels, columns), jnp.bfloat16),
            pltpu.VMEM((2, channels, columns), jnp.bfloat16),
            pltpu.VMEM((height + 2, channels, wide), jnp.bfloat16),
            pltpu.VMEM((channels, height * columns), jnp.bfloat16),
            pltpu.SemaphoreType.DMA((N_COPIES,)),
            pltpu.SemaphoreType.DMA((N_COPIES,)),
        ],
        compiler_params=pltpu.CompilerParams(
            collective_id=0, has_side_effects=True, vmem_limit_bytes=48 * 1024 * 1024
        ),
        cost_estimate=pl.CostEstimate(
            flops=4 * 10**9, bytes_accessed=2 * 10**6, transcendentals=4096
        ),
    )(
        feat,
        offsets[0],
        fractions[0],
        tissue[0],
        w_first.reshape(-1, w_first.shape[-1]),
        w_second.reshape(-1, w_second.shape[-1]),
        head_weight,
    )
    return (jnp.transpose(warped, (1, 0, 2))[None], motion[None])


def solution(mesh):
    tile = P("pair", None, "row", "col")
    return jax.shard_map(
        functools.partial(shards, mesh.shape["row"], mesh.shape["col"]),
        mesh=mesh,
        in_specs=(tile, tile, tile, P("pair", "row", "col"), P(), P(), P()),
        out_specs=(tile, tile),
        check_vma=False,
    )
```

```python
import functools

import jax
import jax.numpy as jnp
from jax import lax
from jax.experimental import pallas as pl
from jax.experimental.pallas import tpu as pltpu
from jax.sharding import PartitionSpec as P

MAXS = 8
BLK = 8
MARGIN = MAXS + 1
FRAC_SCALE = 256.0
STRIP = 16
MESH = pl.DeviceIdType.MESH

STRIPS = [(dr, dc) for dr in (-1, 0, 1) for dc in (-1, 1)]
N_COPIES = 16
CHUNKS = 4


def lanes(shape):
    return lax.broadcasted_iota(jnp.int32, shape, len(shape) - 1)


def kernel(
    n_row,
    n_col,
    feat_in,
    offsets_in,
    fractions_in,
    w_first_in,
    w_second_in,
    tissue,
    head,
    out,
    motion_out,
    own,
    other,
    packed,
    strips,
    package,
    hidden,
    hidden_two,
    partial,
    flat,
    feat,
    feat_here,
    offsets,
    fractions,
    w_first,
    w_second,
    send_sem,
    recv_sem,
    load_sem,
):
    height, channels, columns = feat.shape
    loads = [
        pltpu.make_async_copy(source, target, load_sem.at[n])
        for n, (source, target) in enumerate(
            (
                (feat_in, feat_here),
                (w_first_in, w_first),
                (w_second_in, w_second),
                (offsets_in, offsets),
                (fractions_in, fractions),
            )
        )
    ]
    for load in loads:
        load.start()
    slots = columns // STRIP
    pair = lax.axis_index("pair")
    row = lax.axis_index("row")
    col = lax.axis_index("col")

    def exists(dr, dc):
        ok = None
        for test in (
            [row + dr >= 0, row + dr < n_row] if dr else []
        ) + ([col + dc >= 0, col + dc < n_col] if dc else []):
            ok = test if ok is None else jnp.logical_and(ok, test)
        return ok

    neighbours = [(dr, dc) for dr in (-1, 0, 1) for dc in (-1, 0, 1) if dr or dc]
    barrier = pltpu.get_barrier_semaphore()
    pl.semaphore_signal(
        barrier, inc=1, device_id=(1 - pair, row, col), device_id_type=MESH
    )
    expected = jnp.int32(1)
    for dr, dc in neighbours:
        here = exists(dr, dc)
        expected = expected + here.astype(jnp.int32)

        @pl.when(here)
        def _():
            pl.semaphore_signal(
                barrier, inc=1, device_id=(pair, row + dr, col + dc), device_id_type=MESH
            )

    loads[0].wait()
    flat[...] = feat_here[...].astype(jnp.float32).reshape(channels * height, columns)

    lane = lanes((channels, columns))
    slot = lane // STRIP
    for plane in range(height // slots):
        first = jnp.zeros((channels, columns), jnp.float32)
        last = first
        for k in range(slots):
            y = plane * slots + k
            value = flat[pl.ds(y, channels, stride=height), :]
            feat[y] = value.astype(jnp.bfloat16)
            if k:
                value = pltpu.roll(value, STRIP * k, 1)
            first = jnp.where(slot == k, value, first)
            last = jnp.where(slot == (k - 1) % slots, value, last)
        packed[0, plane] = first.astype(jnp.bfloat16)
        packed[1, plane] = last.astype(jnp.bfloat16)

    pl.semaphore_wait(barrier, expected)

    def copy(index, source, target, device):
        return pltpu.make_async_remote_copy(
            src_ref=source,
            dst_ref=target,
            send_sem=send_sem.at[index],
            recv_sem=recv_sem.at[index],
            device_id=device,
            device_id_type=MESH,
        )

    partner = (1 - pair, row, col)
    low = pl.ds(0, columns)
    piece = height // CHUNKS
    to_partner = [
        copy(
            12 + n if n else 0,
            feat.at[pl.ds(n * piece, piece)],
            other.at[pl.ds(2 + n * piece, piece), :, low],
            partner,
        )
        for n in range(CHUNKS)
    ]
    near = []
    for n, (dr, dc) in enumerate(STRIPS):
        near.append(
            (
                copy(
                    3 + n,
                    packed.at[0 if dc < 0 else 1],
                    strips.at[n],
                    (pair, row + dr, col + dc),
                ),
                (dr, dc),
                strips.at[n],
            )
        )
    for index, dr, source, target in (
        (1, 1, pl.ds(height - MARGIN, MARGIN), pl.ds(0, MARGIN)),
        (2, -1, pl.ds(0, MARGIN), pl.ds(height + MARGIN, MARGIN)),
    ):
        place = own.at[target, :, low]
        near.append((copy(index, feat.at[source], place, (pair, row + dr, col)), (dr, 0), place))

    for moved, (dr, dc), _ in near:
        pl.when(exists(dr, dc))(moved.start)
    for moved in to_partner:
        moved.start()
    for _, (dr, dc), place in near:

        @pl.when(jnp.logical_not(exists(-dr, -dc)))
        def _():
            place[...] = jnp.zeros(place.shape, place.dtype)

    own[pl.ds(MARGIN, height), :, low] = feat[...]

    for load in loads[1:]:
        load.wait()
    taps = 3 * channels
    w_own, w_other, w_two = (
        jnp.concatenate([ref[pl.ds(taps * a, taps), pl.ds(at, channels)] for a in range(3)], axis=1)
        for ref, at in ((w_first, 0), (w_first, channels), (w_second, 0))
    )

    for moved, (dr, dc), _ in near:
        pl.when(exists(-dr, -dc))(moved.wait_recv)

    bundle = jnp.zeros((channels, columns), jnp.float32)
    for i in range(height + 2 * MARGIN):
        side = -1 if i < MARGIN else (0 if i < MARGIN + height else 1)
        k = i - MARGIN - side * height
        left = strips[STRIPS.index((-side, 1)), k // slots].astype(jnp.float32)
        right = strips[STRIPS.index((-side, -1)), k // slots].astype(jnp.float32)
        k = k % slots
        value = jnp.where(
            slot == k, right, jnp.where(slot == (k - 1) % slots, left, 0.0)
        )
        if k:
            value = pltpu.roll(value, columns - STRIP * k, 1)
        own[i, :, pl.ds(columns, columns)] = value.astype(jnp.bfloat16)
        j = i - MARGIN + 2
        if 0 <= j < height + 4:
            bundle = jnp.where(lane // 4 == j, pltpu.roll(value, 2 + 4 * j, 1), bundle)
    package[0] = bundle.astype(jnp.bfloat16)

    passed = [
        copy(9, package.at[0], package.at[1], partner),
        copy(
            10,
            own.at[pl.ds(MARGIN - 2, 2), :, low],
            other.at[pl.ds(0, 2), :, low],
            partner,
        ),
        copy(
            11,
            own.at[pl.ds(MARGIN + height, 2), :, low],
            other.at[pl.ds(height + 2, 2), :, low],
            partner,
        ),
    ]
    for moved in passed:
        moved.start()
    wide = 2 * columns

    def own_part(step, carry):
        for part in range(6):
            y = step * 6 + part
            window = own[pl.ds(y + MARGIN - 2, 3)].reshape(taps, wide)
            partial[y] = jnp.dot(w_own, window, preferred_element_type=jnp.float32)
        return carry

    lax.fori_loop(0, (height + 2) // 6, own_part, 0)

    passed[0].wait_recv()
    bundle = package[1].astype(jnp.float32)
    for j in range(height + 4):
        other[j, :, pl.ds(columns, columns)] = pltpu.roll(
            bundle, (2 * columns - 2 - 4 * j) % columns, 1
        ).astype(jnp.bfloat16)

    def joined_taps(z):
        return (
            pltpu.roll(z[:channels], 1, 1)
            + z[channels : 2 * channels]
            + pltpu.roll(z[2 * channels :], wide - 1, 1)
        )

    wide_lane = lanes((channels, wide))
    place_col = jnp.where(wide_lane < wide * 3 // 4, wide_lane, wide_lane - wide) + col * columns
    col_ok = jnp.logical_and(place_col >= 0, place_col < n_col * columns)

    def first_layer(y):
        window = other[pl.ds(y, 3)].reshape(taps, wide)
        value = joined_taps(
            partial[y] + jnp.dot(w_other, window, preferred_element_type=jnp.float32)
        )
        if y == 0:
            ok = jnp.logical_and(col_ok, row > 0)
        elif y == height + 1:
            ok = jnp.logical_and(col_ok, row < n_row - 1)
        else:
            ok = col_ok
        hidden[y] = jnp.where(ok, jnp.maximum(value, 0.0), 0.0).astype(jnp.bfloat16)

    passed[1].wait_recv()
    for n in range(CHUNKS):
        to_partner[n].wait_recv()
        for y in range(n * piece, (n + 1) * piece):
            first_layer(y)
    passed[2].wait_recv()
    for y in range(height, height + 2):
        first_layer(y)

    for y in range(height):
        window = hidden[pl.ds(y, 3)].reshape(taps, wide)
        value = joined_taps(jnp.dot(w_two, window, preferred_element_type=jnp.float32))
        hidden_two[:, pl.ds(y * columns, columns)] = jnp.maximum(value[:, :columns], 0.0).astype(
            jnp.bfloat16
        )

    residual = jnp.tanh(
        jnp.dot(head[...], hidden_two[...], preferred_element_type=jnp.float32)
    )
    cells = columns // BLK
    spread = (
        lax.broadcasted_iota(jnp.int32, (cells, columns), 1) // BLK
        == lax.broadcasted_iota(jnp.int32, (cells, columns), 0)
    ).astype(jnp.bfloat16)
    coverage = jnp.dot(
        tissue[...].astype(jnp.float32).astype(jnp.bfloat16),
        spread,
        preferred_element_type=jnp.float32,
    )
    for y in range(height):
        cover = coverage[y // BLK : y // BLK + 1]
        for k in range(2):
            motion_out[k, pl.ds(y, 1), :] = (
                offsets[k, pl.ds(y, 1), :].astype(jnp.float32)
                + fractions[k, pl.ds(y, 1), :].astype(jnp.float32) / FRAC_SCALE
                + cover * residual[k : k + 1, y * columns : (y + 1) * columns]
            )

    depth = 2 * MARGIN + 2
    source = lax.broadcasted_iota(jnp.int32, (wide, wide), 0)
    source = jnp.where(source < wide * 3 // 4, source, source - wide).astype(jnp.float32)
    target = lanes((1, wide))
    target_col = (target % columns).astype(jnp.float32)
    target_row = (target // columns).astype(jnp.float32)
    reach = lax.broadcasted_iota(jnp.int32, (depth, wide), 0).astype(jnp.float32) - MARGIN

    def warp(y):
        both = [
            jnp.concatenate(
                [motion_out[k, pl.ds(y, 1), :], motion_out[k, pl.ds(y + 1, 1), :]], axis=1
            )
            for k in range(2)
        ]
        col_weight = jnp.maximum(1.0 - jnp.abs(both[1] + target_col - source), 0.0)
        row_weight = jnp.maximum(1.0 - jnp.abs(both[0] + target_row - reach), 0.0)
        rows = own[pl.ds(y, depth)].reshape(depth * channels, wide)
        picked = jnp.dot(
            rows, col_weight.astype(jnp.bfloat16), preferred_element_type=jnp.float32
        )
        total = None
        for d in range(depth):
            term = picked[d * channels : (d + 1) * channels] * row_weight[d : d + 1]
            total = term if total is None else total + term
        flat[pl.ds(y, channels, stride=height), :] = total[:, :columns]
        flat[pl.ds(y + 1, channels, stride=height), :] = total[:, columns:]

    def warp_four(t, carry):
        warp(4 * t)
        warp(4 * t + 2)
        return carry

    lax.fori_loop(0, height // 4, warp_four, 0)
    out[...] = flat[...].reshape(channels, height, columns).astype(jnp.bfloat16)

    for moved, (dr, dc), _ in near:
        pl.when(exists(dr, dc))(moved.wait_send)
    for moved in to_partner + passed:
        moved.wait_send()


def shards(n_row, n_col, features, offsets, fractions, tissue, w_first, w_second, head_weight):
    _, channels, height, columns = features.shape
    wide = 2 * columns
    vmem = pl.BlockSpec(memory_space=pltpu.VMEM)
    warped, motion = pl.pallas_call(
        functools.partial(kernel, n_row, n_col),
        out_shape=(
            jax.ShapeDtypeStruct((channels, height, columns), jnp.bfloat16),
            jax.ShapeDtypeStruct((2, height, columns), jnp.float32),
        ),
        in_specs=[pl.BlockSpec(memory_space=pltpu.HBM)] * 5 + [vmem] * 2,
        out_specs=(vmem, vmem),
        scratch_shapes=[
            pltpu.VMEM((height + 2 * MARGIN, channels, wide), jnp.bfloat16),
            pltpu.VMEM((height + 4, channels, wide), jnp.bfloat16),
            pltpu.VMEM((2, 2, channels, columns), jnp.bfloat16),
            pltpu.VMEM((6, 2, channels, columns), jnp.bfloat16),
            pltpu.VMEM((2, channels, columns), jnp.bfloat16),
            pltpu.VMEM((height + 2, channels, wide), jnp.bfloat16),
            pltpu.VMEM((channels, height * columns), jnp.bfloat16),
            pltpu.VMEM((height + 2, 3 * channels, wide), jnp.float32),
            pltpu.VMEM((channels * height, columns), jnp.float32),
            pltpu.VMEM((height, channels, columns), jnp.bfloat16),
            pltpu.VMEM((channels, height, columns), jnp.bfloat16),
            pltpu.VMEM((2, height, columns), jnp.int32),
            pltpu.VMEM((2, height, columns), jnp.int32),
            pltpu.VMEM((9 * channels, 2 * channels), jnp.bfloat16),
            pltpu.VMEM((9 * channels, channels), jnp.bfloat16),
            pltpu.SemaphoreType.DMA((N_COPIES,)),
            pltpu.SemaphoreType.DMA((N_COPIES,)),
            pltpu.SemaphoreType.DMA((5,)),
        ],
        compiler_params=pltpu.CompilerParams(
            collective_id=0, has_side_effects=True, vmem_limit_bytes=63 * 1024 * 1024
        ),
        cost_estimate=pl.CostEstimate(
            flops=4 * 10**9, bytes_accessed=2 * 10**6, transcendentals=4096
        ),
    )(
        features[0],
        offsets[0],
        fractions[0],
        w_first.reshape(-1, w_first.shape[-1]),
        w_second.reshape(-1, w_second.shape[-1]),
        tissue[0],
        head_weight,
    )
    return (warped[None], motion[None])


def solution(mesh):
    tile = P("pair", None, "row", "col")
    return jax.shard_map(
        functools.partial(shards, mesh.shape["row"], mesh.shape["col"]),
        mesh=mesh,
        in_specs=(tile, tile, tile, P("pair", "row", "col"), P(), P(), P()),
        out_specs=(tile, tile),
        check_vma=False,
    )
```

```python
import functools

import jax
import jax.numpy as jnp
from jax import lax
from jax.experimental import pallas as pl
from jax.experimental.pallas import tpu as pltpu
from jax.sharding import PartitionSpec as P

MAXS = 8
BLK = 8
MARGIN = MAXS + 1
FRAC_SCALE = 256.0
STRIP = 16
MESH = pl.DeviceIdType.MESH

STRIPS = [(dr, dc) for dr in (-1, 0, 1) for dc in (-1, 1)]
N_COPIES = 14
CHUNKS = 2


def lanes(shape):
    return lax.broadcasted_iota(jnp.int32, shape, len(shape) - 1)


def kernel(
    n_row,
    n_col,
    feat_in,
    offsets_in,
    fractions_in,
    w_first_in,
    w_second_in,
    tissue,
    head,
    out,
    motion_out,
    own,
    other,
    packed,
    strips,
    package,
    hidden,
    hidden_two,
    partial,
    residual,
    flat,
    feat,
    feat_here,
    offsets,
    fractions,
    w_first,
    w_second,
    send_sem,
    recv_sem,
    load_sem,
):
    height, channels, columns = feat.shape
    half = height // 2
    loads = [
        pltpu.make_async_copy(source, target, load_sem.at[n])
        for n, (source, target) in enumerate(
            (
                (feat_in, feat_here),
                (w_first_in, w_first),
                (w_second_in, w_second),
                (offsets_in, offsets),
                (fractions_in, fractions),
            )
        )
    ]
    for load in loads:
        load.start()
    slots = columns // STRIP
    pair = lax.axis_index("pair")
    row = lax.axis_index("row")
    col = lax.axis_index("col")

    def exists(dr, dc):
        ok = None
        for test in (
            [row + dr >= 0, row + dr < n_row] if dr else []
        ) + ([col + dc >= 0, col + dc < n_col] if dc else []):
            ok = test if ok is None else jnp.logical_and(ok, test)
        return ok

    neighbours = [(dr, dc) for dr in (-1, 0, 1) for dc in (-1, 0, 1) if dr or dc]
    barrier = pltpu.get_barrier_semaphore()
    pl.semaphore_signal(
        barrier, inc=1, device_id=(1 - pair, row, col), device_id_type=MESH
    )
    expected = jnp.int32(1)
    for dr, dc in neighbours:
        here = exists(dr, dc)
        expected = expected + here.astype(jnp.int32)

        @pl.when(here)
        def _():
            pl.semaphore_signal(
                barrier, inc=1, device_id=(pair, row + dr, col + dc), device_id_type=MESH
            )

    loads[0].wait()
    flat[...] = feat_here[...].astype(jnp.float32).reshape(channels * height, columns)

    lane = lanes((channels, columns))
    slot = lane // STRIP
    for plane in range(height // slots):
        first = jnp.zeros((channels, columns), jnp.float32)
        last = first
        for k in range(slots):
            y = plane * slots + k
            value = flat[pl.ds(y, channels, stride=height), :]
            feat[y] = value.astype(jnp.bfloat16)
            if k:
                value = pltpu.roll(value, STRIP * k, 1)
            first = jnp.where(slot == k, value, first)
            last = jnp.where(slot == (k - 1) % slots, value, last)
        packed[0, plane] = first.astype(jnp.bfloat16)
        packed[1, plane] = last.astype(jnp.bfloat16)

    pl.semaphore_wait(barrier, expected)

    def copy(index, source, target, device):
        return pltpu.make_async_remote_copy(
            src_ref=source,
            dst_ref=target,
            send_sem=send_sem.at[index],
            recv_sem=recv_sem.at[index],
            device_id=device,
            device_id_type=MESH,
        )

    partner = (1 - pair, row, col)
    low = pl.ds(0, columns)
    top = pl.multiple_of(pair * half, half)
    top_there = pl.multiple_of((1 - pair) * half, half)
    body = half + 2
    piece = body // CHUNKS
    to_partner = [
        copy(
            12 + n if n else 0,
            feat.at[pl.ds((1 - pair) * (height - body) + n * piece, piece)],
            other.at[pl.ds(2 * pair + n * piece, piece), :, low],
            partner,
        )
        for n in range(CHUNKS)
    ]
    near = []
    for n, (dr, dc) in enumerate(STRIPS):
        near.append(
            (
                copy(
                    3 + n,
                    packed.at[0 if dc < 0 else 1],
                    strips.at[n],
                    (pair, row + dr, col + dc),
                ),
                (dr, dc),
                strips.at[n],
            )
        )
    for index, dr, source, target in (
        (1, 1, pl.ds(height - MARGIN, MARGIN), pl.ds(0, MARGIN)),
        (2, -1, pl.ds(0, MARGIN), pl.ds(height + MARGIN, MARGIN)),
    ):
        place = own.at[target, :, low]
        near.append((copy(index, feat.at[source], place, (pair, row + dr, col)), (dr, 0), place))

    for moved, (dr, dc), _ in near:
        pl.when(exists(dr, dc))(moved.start)
    for moved in to_partner:
        moved.start()
    for _, (dr, dc), place in near:

        @pl.when(jnp.logical_not(exists(-dr, -dc)))
        def _():
            place[...] = jnp.zeros(place.shape, place.dtype)

    own[pl.ds(MARGIN, height), :, low] = feat[...]

    for load in loads[1:]:
        load.wait()
    taps = 3 * channels
    w_self, w_cross, w_two = (
        jnp.concatenate([ref[pl.ds(taps * a, taps), pl.ds(at, channels)] for a in range(3)], axis=1)
        for ref, at in ((w_first, 0), (w_first, channels), (w_second, 0))
    )
    w_own = jnp.concatenate([w_self, w_cross], axis=0)
    w_other = jnp.concatenate([w_cross, w_self], axis=0)

    for moved, (dr, dc), _ in near:
        pl.when(exists(-dr, -dc))(moved.wait_recv)

    bundle = jnp.zeros((channels, columns), jnp.float32)
    for i in range(height + 2 * MARGIN):
        side = -1 if i < MARGIN else (0 if i < MARGIN + height else 1)
        k = i - MARGIN - side * height
        left = strips[STRIPS.index((-side, 1)), k // slots].astype(jnp.float32)
        right = strips[STRIPS.index((-side, -1)), k // slots].astype(jnp.float32)
        k = k % slots
        value = jnp.where(
            slot == k, right, jnp.where(slot == (k - 1) % slots, left, 0.0)
        )
        if k:
            value = pltpu.roll(value, columns - STRIP * k, 1)
        own[i, :, pl.ds(columns, columns)] = value.astype(jnp.bfloat16)
        j = i - MARGIN + 2
        if 0 <= j < height + 4:
            bundle = jnp.where(lane // 4 == j, pltpu.roll(value, 2 + 4 * j, 1), bundle)
    package[0] = bundle.astype(jnp.bfloat16)

    passed = [
        copy(9, package.at[0], package.at[1], partner),
        copy(
            10,
            own.at[pl.ds(MARGIN - 2 + (1 - pair) * (height + 2), 2), :, low],
            other.at[pl.ds((1 - pair) * body, 2), :, low],
            partner,
        ),
    ]
    for moved in passed:
        moved.start()
    wide = 2 * columns

    def own_part(step, carry):
        for part in range(5):
            y = step * 5 + part
            window = own[pl.ds(top + y + MARGIN - 2, 3)].reshape(taps, wide)
            partial[y] = jnp.dot(w_own, window, preferred_element_type=jnp.float32)
        return carry

    lax.fori_loop(0, (half + 2) // 5, own_part, 0)

    passed[0].wait_recv()
    bundle = package[1].astype(jnp.float32)
    bundle = jnp.where(pair == 0, bundle, pltpu.roll(bundle, columns - 4 * half, 1))
    for j in range(half + 4):
        other[j, :, pl.ds(columns, columns)] = pltpu.roll(
            bundle, (2 * columns - 2 - 4 * j) % columns, 1
        ).astype(jnp.bfloat16)

    def joined_taps(z):
        return (
            pltpu.roll(z[:channels], 1, 1)
            + z[channels : 2 * channels]
            + pltpu.roll(z[2 * channels :], wide - 1, 1)
        )

    wide_lane = lanes((channels, wide))
    place_col = jnp.where(wide_lane < wide * 3 // 4, wide_lane, wide_lane - wide) + col * columns
    col_ok = jnp.logical_and(place_col >= 0, place_col < n_col * columns)

    def first_layer(y):
        window = other[pl.ds(y, 3)].reshape(taps, wide)
        both = partial[y] + jnp.dot(w_other, window, preferred_element_type=jnp.float32)
        if y == 0:
            ok = jnp.logical_and(col_ok, row * height + top > 0)
        elif y == half + 1:
            ok = jnp.logical_and(col_ok, row * height + top + half < n_row * height)
        else:
            ok = col_ok
        for section in range(2):
            value = joined_taps(both[section * taps : (section + 1) * taps])
            hidden[section, y] = jnp.where(ok, jnp.maximum(value, 0.0), 0.0).astype(jnp.bfloat16)

    passed[1].wait_recv()
    to_partner[0].wait_recv()
    for y in range(piece - 2):
        first_layer(y)
    for moved in to_partner[1:]:
        moved.wait_recv()
    for y in range(piece - 2, half + 2):
        first_layer(y)

    back = copy(11, residual.at[1], residual.at[2], partner)
    for section in (1, 0):
        for y in range(half):
            window = hidden[section, pl.ds(y, 3)].reshape(taps, wide)
            value = joined_taps(jnp.dot(w_two, window, preferred_element_type=jnp.float32))
            hidden_two[:, pl.ds(y * columns, columns)] = jnp.maximum(
                value[:, :columns], 0.0
            ).astype(jnp.bfloat16)
        value = jnp.tanh(jnp.dot(head[...], hidden_two[...], preferred_element_type=jnp.float32))
        for y in range(half):
            for k in range(2):
                residual[section, k, pl.ds(y, 1), :] = value[
                    k : k + 1, y * columns : (y + 1) * columns
                ]
        if section:
            back.start()

    cells = columns // BLK
    spread = (
        lax.broadcasted_iota(jnp.int32, (cells, columns), 1) // BLK
        == lax.broadcasted_iota(jnp.int32, (cells, columns), 0)
    ).astype(jnp.bfloat16)
    coverage = jnp.dot(
        tissue[...].astype(jnp.float32).astype(jnp.bfloat16),
        spread,
        preferred_element_type=jnp.float32,
    )

    def move(start, place, upper):
        cover = [
            jnp.broadcast_to(
                jnp.where(
                    upper, coverage[n : n + 1], coverage[half // BLK + n : half // BLK + n + 1]
                ),
                (BLK, columns),
            )
            for n in range(half // BLK)
        ]
        cover = jnp.concatenate(cover, axis=0) if len(cover) > 1 else cover[0]
        rows = pl.ds(start, half)
        for k in range(2):
            motion_out[k, rows, :] = (
                offsets[k, rows, :].astype(jnp.float32)
                + fractions[k, rows, :].astype(jnp.float32) / FRAC_SCALE
                + cover * residual[place, k]
            )

    depth = 2 * MARGIN + 2
    source = lax.broadcasted_iota(jnp.int32, (wide, wide), 0)
    source = jnp.where(source < wide * 3 // 4, source, source - wide).astype(jnp.float32)
    target = lanes((1, wide))
    target_col = (target % columns).astype(jnp.float32)
    target_row = (target // columns).astype(jnp.float32)
    reach = lax.broadcasted_iota(jnp.int32, (depth, wide), 0).astype(jnp.float32) - MARGIN

    def warp(y):
        both = [
            jnp.concatenate(
                [motion_out[k, pl.ds(y, 1), :], motion_out[k, pl.ds(y + 1, 1), :]], axis=1
            )
            for k in range(2)
        ]
        col_weight = jnp.maximum(1.0 - jnp.abs(both[1] + target_col - source), 0.0)
        row_weight = jnp.maximum(1.0 - jnp.abs(both[0] + target_row - reach), 0.0)
        rows = own[pl.ds(y, depth)].reshape(depth * channels, wide)
        picked = jnp.dot(
            rows, col_weight.astype(jnp.bfloat16), preferred_element_type=jnp.float32
        )
        total = None
        for d in range(depth):
            term = picked[d * channels : (d + 1) * channels] * row_weight[d : d + 1]
            total = term if total is None else total + term
        flat[pl.ds(y, channels, stride=height), :] = total[:, :columns]
        flat[pl.ds(y + 1, channels, stride=height), :] = total[:, columns:]

    for start, place, upper in ((top, 0, pair == 0), (top_there, 2, pair != 0)):
        if place:
            back.wait_recv()
        move(start, place, upper)

        def warp_four(t, carry):
            warp(start + 4 * t)
            warp(start + 4 * t + 2)
            return carry

        lax.fori_loop(0, half // 4, warp_four, 0)
    out[...] = flat[...].reshape(channels, height, columns).astype(jnp.bfloat16)

    for moved, (dr, dc), _ in near:
        pl.when(exists(dr, dc))(moved.wait_send)
    for moved in to_partner + passed + [back]:
        moved.wait_send()


def shards(n_row, n_col, features, offsets, fractions, tissue, w_first, w_second, head_weight):
    _, channels, height, columns = features.shape
    wide = 2 * columns
    vmem = pl.BlockSpec(memory_space=pltpu.VMEM)
    warped, motion = pl.pallas_call(
        functools.partial(kernel, n_row, n_col),
        out_shape=(
            jax.ShapeDtypeStruct((channels, height, columns), jnp.bfloat16),
            jax.ShapeDtypeStruct((2, height, columns), jnp.float32),
        ),
        in_specs=[pl.BlockSpec(memory_space=pltpu.HBM)] * 5 + [vmem] * 2,
        out_specs=(vmem, vmem),
        scratch_shapes=[
            pltpu.VMEM((height + 2 * MARGIN, channels, wide), jnp.bfloat16),
            pltpu.VMEM((height // 2 + 4, channels, wide), jnp.bfloat16),
            pltpu.VMEM((2, 2, channels, columns), jnp.bfloat16),
            pltpu.VMEM((6, 2, channels, columns), jnp.bfloat16),
            pltpu.VMEM((2, channels, columns), jnp.bfloat16),
            pltpu.VMEM((2, height // 2 + 2, channels, wide), jnp.bfloat16),
            pltpu.VMEM((channels, height // 2 * columns), jnp.bfloat16),
            pltpu.VMEM((height // 2 + 2, 6 * channels, wide), jnp.float32),
            pltpu.VMEM((3, 2, height // 2, columns), jnp.float32),
            pltpu.VMEM((channels * height, columns), jnp.float32),
            pltpu.VMEM((height, channels, columns), jnp.bfloat16),
            pltpu.VMEM((channels, height, columns), jnp.bfloat16),
            pltpu.VMEM((2, height, columns), jnp.int32),
            pltpu.VMEM((2, height, columns), jnp.int32),
            pltpu.VMEM((9 * channels, 2 * channels), jnp.bfloat16),
            pltpu.VMEM((9 * channels, channels), jnp.bfloat16),
            pltpu.SemaphoreType.DMA((N_COPIES,)),
            pltpu.SemaphoreType.DMA((N_COPIES,)),
            pltpu.SemaphoreType.DMA((5,)),
        ],
        compiler_params=pltpu.CompilerParams(
            collective_id=0, has_side_effects=True, vmem_limit_bytes=63 * 1024 * 1024
        ),
        cost_estimate=pl.CostEstimate(
            flops=4 * 10**9, bytes_accessed=2 * 10**6, transcendentals=4096
        ),
    )(
        features[0],
        offsets[0],
        fractions[0],
        w_first.reshape(-1, w_first.shape[-1]),
        w_second.reshape(-1, w_second.shape[-1]),
        tissue[0],
        head_weight,
    )
    return (warped[None], motion[None])


def solution(mesh):
    tile = P("pair", None, "row", "col")
    return jax.shard_map(
        functools.partial(shards, mesh.shape["row"], mesh.shape["col"]),
        mesh=mesh,
        in_specs=(tile, tile, tile, P("pair", "row", "col"), P(), P(), P()),
        out_specs=(tile, tile),
        check_vma=False,
    )
```

```python
import functools

import jax
import jax.numpy as jnp
from jax import lax
from jax.experimental import pallas as pl
from jax.experimental.pallas import tpu as pltpu
from jax.sharding import PartitionSpec as P

MAXS = 8
BLK = 8
MARGIN = MAXS + 1
FRAC_SCALE = 256.0
STRIP = 16
MESH = pl.DeviceIdType.MESH

STRIPS = [(dr, dc) for dr in (-1, 0, 1) for dc in (-1, 1)]
N_COPIES = 14
CHUNKS = 2


def lanes(shape):
    return lax.broadcasted_iota(jnp.int32, shape, len(shape) - 1)


def kernel(
    n_row,
    n_col,
    feat_in,
    offsets_in,
    fractions_in,
    w_first_in,
    w_second_in,
    tissue,
    head,
    out,
    motion_out,
    own,
    other,
    packed,
    strips,
    package,
    hidden,
    hidden_two,
    partial,
    residual,
    flat,
    feat,
    feat_here,
    offsets,
    fractions,
    w_first,
    w_second,
    send_sem,
    recv_sem,
    load_sem,
):
    height, channels, columns = feat.shape
    half = height // 2
    loads = [
        pltpu.make_async_copy(source, target, load_sem.at[n])
        for n, (source, target) in enumerate(
            (
                (feat_in, feat_here),
                (w_first_in, w_first),
                (w_second_in, w_second),
                (offsets_in, offsets),
                (fractions_in, fractions),
            )
        )
    ]
    for load in loads:
        load.start()
    slots = columns // STRIP
    pair = lax.axis_index("pair")
    row = lax.axis_index("row")
    col = lax.axis_index("col")

    def exists(dr, dc):
        ok = None
        for test in (
            [row + dr >= 0, row + dr < n_row] if dr else []
        ) + ([col + dc >= 0, col + dc < n_col] if dc else []):
            ok = test if ok is None else jnp.logical_and(ok, test)
        return ok

    neighbours = [(dr, dc) for dr in (-1, 0, 1) for dc in (-1, 0, 1) if dr or dc]
    barrier = pltpu.get_barrier_semaphore()
    pl.semaphore_signal(
        barrier, inc=1, device_id=(1 - pair, row, col), device_id_type=MESH
    )
    expected = jnp.int32(1)
    for dr, dc in neighbours:
        here = exists(dr, dc)
        expected = expected + here.astype(jnp.int32)

        @pl.when(here)
        def _():
            pl.semaphore_signal(
                barrier, inc=1, device_id=(pair, row + dr, col + dc), device_id_type=MESH
            )

    loads[0].wait()
    flat[...] = feat_here[...].astype(jnp.float32).reshape(channels * height, columns)

    lane = lanes((channels, columns))
    slot = lane // STRIP
    for plane in range(height // slots):
        first = jnp.zeros((channels, columns), jnp.float32)
        last = first
        for k in range(slots):
            y = plane * slots + k
            value = flat[pl.ds(y, channels, stride=height), :]
            feat[y] = value.astype(jnp.bfloat16)
            if k:
                value = pltpu.roll(value, STRIP * k, 1)
            first = jnp.where(slot == k, value, first)
            last = jnp.where(slot == (k - 1) % slots, value, last)
        packed[0, plane] = first.astype(jnp.bfloat16)
        packed[1, plane] = last.astype(jnp.bfloat16)

    pl.semaphore_wait(barrier, expected)

    def copy(index, source, target, device):
        return pltpu.make_async_remote_copy(
            src_ref=source,
            dst_ref=target,
            send_sem=send_sem.at[index],
            recv_sem=recv_sem.at[index],
            device_id=device,
            device_id_type=MESH,
        )

    partner = (1 - pair, row, col)
    low = pl.ds(0, columns)
    top = pl.multiple_of(pair * half, half)
    top_there = pl.multiple_of((1 - pair) * half, half)
    body = half + 2
    piece = body // CHUNKS
    to_partner = [
        copy(
            12 + n if n else 0,
            feat.at[pl.ds((1 - pair) * (height - body) + n * piece, piece)],
            other.at[pl.ds(2 * pair + n * piece, piece), :, low],
            partner,
        )
        for n in range(CHUNKS)
    ]
    near = []
    for n, (dr, dc) in enumerate(STRIPS):
        near.append(
            (
                copy(
                    3 + n,
                    packed.at[0 if dc < 0 else 1],
                    strips.at[n],
                    (pair, row + dr, col + dc),
                ),
                (dr, dc),
                strips.at[n],
            )
        )
    for index, dr, source, target in (
        (1, 1, pl.ds(height - MARGIN, MARGIN), pl.ds(0, MARGIN)),
        (2, -1, pl.ds(0, MARGIN), pl.ds(height + MARGIN, MARGIN)),
    ):
        place = own.at[target, :, low]
        near.append((copy(index, feat.at[source], place, (pair, row + dr, col)), (dr, 0), place))

    for moved, (dr, dc), _ in near:
        pl.when(exists(dr, dc))(moved.start)
    for moved in to_partner:
        moved.start()
    for _, (dr, dc), place in near:

        @pl.when(jnp.logical_not(exists(-dr, -dc)))
        def _():
            place[...] = jnp.zeros(place.shape, place.dtype)

    own[pl.ds(MARGIN, height), :, low] = feat[...]

    for load in loads[1:]:
        load.wait()
    taps = 3 * channels
    w_self, w_cross, w_two = (
        jnp.concatenate([ref[pl.ds(taps * a, taps), pl.ds(at, channels)] for a in range(3)], axis=1)
        for ref, at in ((w_first, 0), (w_first, channels), (w_second, 0))
    )
    w_own = jnp.concatenate([w_self, w_cross], axis=0)
    w_other = jnp.concatenate([w_cross, w_self], axis=0)

    for moved, (dr, dc), _ in near:
        pl.when(exists(-dr, -dc))(moved.wait_recv)

    bundle = jnp.zeros((channels, columns), jnp.float32)
    for i in range(height + 2 * MARGIN):
        side = -1 if i < MARGIN else (0 if i < MARGIN + height else 1)
        k = i - MARGIN - side * height
        left = strips[STRIPS.index((-side, 1)), k // slots].astype(jnp.float32)
        right = strips[STRIPS.index((-side, -1)), k // slots].astype(jnp.float32)
        k = k % slots
        value = jnp.where(
            slot == k, right, jnp.where(slot == (k - 1) % slots, left, 0.0)
        )
        if k:
            value = pltpu.roll(value, columns - STRIP * k, 1)
        own[i, :, pl.ds(columns, columns)] = value.astype(jnp.bfloat16)
        j = i - MARGIN + 2
        if 0 <= j < height + 4:
            bundle = jnp.where(lane // 4 == j, pltpu.roll(value, 2 + 4 * j, 1), bundle)
    package[0] = bundle.astype(jnp.bfloat16)

    passed = [
        copy(9, package.at[0], package.at[1], partner),
        copy(
            10,
            own.at[pl.ds(MARGIN - 2 + (1 - pair) * (height + 2), 2), :, low],
            other.at[pl.ds((1 - pair) * body, 2), :, low],
            partner,
        ),
    ]
    for moved in passed:
        moved.start()
    wide = 2 * columns

    def own_part(step, carry):
        for part in range(5):
            y = step * 5 + part
            window = own[pl.ds(top + y + MARGIN - 2, 3)].reshape(taps, wide)
            partial[y] = jnp.dot(w_own, window, preferred_element_type=jnp.float32)
        return carry

    lax.fori_loop(0, (half + 2) // 5, own_part, 0)

    passed[0].wait_recv()
    bundle = package[1].astype(jnp.float32)
    bundle = jnp.where(pair == 0, bundle, pltpu.roll(bundle, columns - 4 * half, 1))
    for j in range(half + 4):
        other[j, :, pl.ds(columns, columns)] = pltpu.roll(
            bundle, (2 * columns - 2 - 4 * j) % columns, 1
        ).astype(jnp.bfloat16)

    def joined_taps(z):
        return (
            pltpu.roll(z[:channels], 1, 1)
            + z[channels : 2 * channels]
            + pltpu.roll(z[2 * channels :], wide - 1, 1)
        )

    wide_lane = lanes((channels, wide))
    place_col = jnp.where(wide_lane < wide * 3 // 4, wide_lane, wide_lane - wide) + col * columns
    col_ok = jnp.logical_and(place_col >= 0, place_col < n_col * columns)

    def first_layer(y):
        window = other[pl.ds(y, 3)].reshape(taps, wide)
        both = partial[y] + jnp.dot(w_other, window, preferred_element_type=jnp.float32)
        if y == 0:
            ok = jnp.logical_and(col_ok, row * height + top > 0)
        elif y == half + 1:
            ok = jnp.logical_and(col_ok, row * height + top + half < n_row * height)
        else:
            ok = col_ok
        for section in range(2):
            value = joined_taps(both[section * taps : (section + 1) * taps])
            hidden[section, y] = jnp.where(ok, jnp.maximum(value, 0.0), 0.0).astype(jnp.bfloat16)

    passed[1].wait_recv()
    to_partner[0].wait_recv()
    for y in range(piece - 2):
        first_layer(y)
    for moved in to_partner[1:]:
        moved.wait_recv()
    for y in range(piece - 2, half + 2):
        first_layer(y)

    back = copy(11, residual.at[1], residual.at[2], partner)
    for section in (1, 0):
        for y in range(half):
            window = hidden[section, pl.ds(y, 3)].reshape(taps, wide)
            value = joined_taps(jnp.dot(w_two, window, preferred_element_type=jnp.float32))
            hidden_two[:, pl.ds(y * columns, columns)] = jnp.maximum(
                value[:, :columns], 0.0
            ).astype(jnp.bfloat16)
        value = jnp.tanh(jnp.dot(head[...], hidden_two[...], preferred_element_type=jnp.float32))
        for y in range(half):
            for k in range(2):
                residual[section, k, pl.ds(y, 1), :] = value[
                    k : k + 1, y * columns : (y + 1) * columns
                ]
        if section:
            back.start()

    cells = columns // BLK
    spread = (
        lax.broadcasted_iota(jnp.int32, (cells, columns), 1) // BLK
        == lax.broadcasted_iota(jnp.int32, (cells, columns), 0)
    ).astype(jnp.bfloat16)
    coverage = jnp.dot(
        tissue[...].astype(jnp.float32).astype(jnp.bfloat16),
        spread,
        preferred_element_type=jnp.float32,
    )

    def move(start, place, upper):
        cover = [
            jnp.broadcast_to(
                jnp.where(
                    upper, coverage[n : n + 1], coverage[half // BLK + n : half // BLK + n + 1]
                ),
                (BLK, columns),
            )
            for n in range(half // BLK)
        ]
        cover = jnp.concatenate(cover, axis=0) if len(cover) > 1 else cover[0]
        rows = pl.ds(start, half)
        for k in range(2):
            motion_out[k, rows, :] = (
                offsets[k, rows, :].astype(jnp.float32)
                + fractions[k, rows, :].astype(jnp.float32) / FRAC_SCALE
                + cover * residual[place, k]
            )

    depth = 2 * MARGIN + 2
    source = lax.broadcasted_iota(jnp.int32, (wide, wide), 0)
    source = jnp.where(source < wide * 3 // 4, source, source - wide).astype(jnp.float32)
    target = lanes((1, wide))
    target_col = (target % columns).astype(jnp.float32)
    target_row = (target // columns).astype(jnp.float32)
    reach = lax.broadcasted_iota(jnp.int32, (depth, wide), 0).astype(jnp.float32) - MARGIN

    def warp(y):
        both = [
            jnp.concatenate(
                [motion_out[k, pl.ds(y, 1), :], motion_out[k, pl.ds(y + 1, 1), :]], axis=1
            )
            for k in range(2)
        ]
        col_weight = jnp.maximum(1.0 - jnp.abs(both[1] + target_col - source), 0.0)
        row_weight = jnp.maximum(1.0 - jnp.abs(both[0] + target_row - reach), 0.0)
        rows = own[pl.ds(y, depth)].reshape(depth * channels, wide)
        picked = jnp.dot(
            rows, col_weight.astype(jnp.bfloat16), preferred_element_type=jnp.float32
        )
        total = None
        for d in range(depth):
            term = picked[d * channels : (d + 1) * channels] * row_weight[d : d + 1]
            total = term if total is None else total + term
        flat[pl.ds(y, channels, stride=height), :] = total[:, :columns]
        flat[pl.ds(y + 1, channels, stride=height), :] = total[:, columns:]

    for start, place, upper in ((top, 0, pair == 0), (top_there, 2, pair != 0)):
        if place:
            back.wait_recv()
        move(start, place, upper)

        def warp_four(t, carry):
            warp(start + 4 * t)
            warp(start + 4 * t + 2)
            return carry

        lax.fori_loop(0, half // 4, warp_four, 0)
    out[...] = flat[...].reshape(channels, height, columns).astype(jnp.bfloat16)

    for moved, (dr, dc), _ in near:
        pl.when(exists(dr, dc))(moved.wait_send)
    for moved in to_partner + passed + [back]:
        moved.wait_send()


def shards(n_row, n_col, features, offsets, fractions, tissue, w_first, w_second, head_weight):
    _, channels, height, columns = features.shape
    wide = 2 * columns
    vmem = pl.BlockSpec(memory_space=pltpu.VMEM)
    warped, motion = pl.pallas_call(
        functools.partial(kernel, n_row, n_col),
        out_shape=(
            pltpu.VMEM((channels, height, columns), jnp.bfloat16),
            pltpu.VMEM((2, height, columns), jnp.float32),
        ),
        in_specs=[pl.BlockSpec(memory_space=pltpu.HBM)] * 5 + [vmem] * 2,
        out_specs=(vmem, vmem),
        scratch_shapes=[
            pltpu.VMEM((height + 2 * MARGIN, channels, wide), jnp.bfloat16),
            pltpu.VMEM((height // 2 + 4, channels, wide), jnp.bfloat16),
            pltpu.VMEM((2, 2, channels, columns), jnp.bfloat16),
            pltpu.VMEM((6, 2, channels, columns), jnp.bfloat16),
            pltpu.VMEM((2, channels, columns), jnp.bfloat16),
            pltpu.VMEM((2, height // 2 + 2, channels, wide), jnp.bfloat16),
            pltpu.VMEM((channels, height // 2 * columns), jnp.bfloat16),
            pltpu.VMEM((height // 2 + 2, 6 * channels, wide), jnp.float32),
            pltpu.VMEM((3, 2, height // 2, columns), jnp.float32),
            pltpu.VMEM((channels * height, columns), jnp.float32),
            pltpu.VMEM((height, channels, columns), jnp.bfloat16),
            pltpu.VMEM((channels, height, columns), jnp.bfloat16),
            pltpu.VMEM((2, height, columns), jnp.int32),
            pltpu.VMEM((2, height, columns), jnp.int32),
            pltpu.VMEM((9 * channels, 2 * channels), jnp.bfloat16),
            pltpu.VMEM((9 * channels, channels), jnp.bfloat16),
            pltpu.SemaphoreType.DMA((N_COPIES,)),
            pltpu.SemaphoreType.DMA((N_COPIES,)),
            pltpu.SemaphoreType.DMA((5,)),
        ],
        compiler_params=pltpu.CompilerParams(
            collective_id=0, has_side_effects=True, vmem_limit_bytes=63 * 1024 * 1024
        ),
        cost_estimate=pl.CostEstimate(
            flops=4 * 10**9, bytes_accessed=2 * 10**6, transcendentals=4096
        ),
    )(
        features[0],
        offsets[0],
        fractions[0],
        w_first.reshape(-1, w_first.shape[-1]),
        w_second.reshape(-1, w_second.shape[-1]),
        tissue[0],
        head_weight,
    )
    return (warped[None], motion[None])


def solution(mesh):
    tile = P("pair", None, "row", "col")
    return jax.shard_map(
        functools.partial(shards, mesh.shape["row"], mesh.shape["col"]),
        mesh=mesh,
        in_specs=(tile, tile, tile, P("pair", "row", "col"), P(), P(), P()),
        out_specs=(tile, tile),
        check_vma=False,
    )
```

```python
import functools

import jax
import jax.numpy as jnp
from jax import lax
from jax.experimental import pallas as pl
from jax.experimental.pallas import tpu as pltpu
from jax.sharding import PartitionSpec as P

MAXS = 8
BLK = 8
MARGIN = MAXS + 1
FRAC_SCALE = 256.0
STRIP = 16
MESH = pl.DeviceIdType.MESH

STRIPS = [(dr, dc) for dr in (-1, 0, 1) for dc in (-1, 1)]
N_COPIES = 14
CHUNKS = 2


def lanes(shape):
    return lax.broadcasted_iota(jnp.int32, shape, len(shape) - 1)


def kernel(
    n_row,
    n_col,
    feat_in,
    offsets_in,
    fractions_in,
    w_first_in,
    w_second_in,
    tissue,
    head,
    out,
    motion_out,
    own,
    other,
    packed,
    strips,
    package,
    hidden,
    hidden_two,
    partial,
    residual,
    flat,
    feat,
    feat_here,
    offsets,
    fractions,
    w_first,
    w_second,
    send_sem,
    recv_sem,
    load_sem,
):
    height, channels, columns = feat.shape
    half = height // 2
    loads = [
        pltpu.make_async_copy(source, target, load_sem.at[n])
        for n, (source, target) in enumerate(
            (
                (feat_in, feat_here),
                (w_first_in, w_first),
                (w_second_in, w_second),
                (offsets_in, offsets),
                (fractions_in, fractions),
            )
        )
    ]
    for load in loads:
        load.start()
    slots = columns // STRIP
    pair = lax.axis_index("pair")
    row = lax.axis_index("row")
    col = lax.axis_index("col")

    def exists(dr, dc):
        ok = None
        for test in (
            [row + dr >= 0, row + dr < n_row] if dr else []
        ) + ([col + dc >= 0, col + dc < n_col] if dc else []):
            ok = test if ok is None else jnp.logical_and(ok, test)
        return ok

    neighbours = [(dr, dc) for dr in (-1, 0, 1) for dc in (-1, 0, 1) if dr or dc]
    barrier = pltpu.get_barrier_semaphore()
    pl.semaphore_signal(
        barrier, inc=1, device_id=(1 - pair, row, col), device_id_type=MESH
    )
    expected = jnp.int32(1)
    for dr, dc in neighbours:
        here = exists(dr, dc)
        expected = expected + here.astype(jnp.int32)

        @pl.when(here)
        def _():
            pl.semaphore_signal(
                barrier, inc=1, device_id=(pair, row + dr, col + dc), device_id_type=MESH
            )

    loads[0].wait()
    flat[...] = feat_here[...].astype(jnp.float32).reshape(channels * height, columns)

    lane = lanes((channels, columns))
    slot = lane // STRIP
    for plane in range(height // slots):
        first = jnp.zeros((channels, columns), jnp.float32)
        last = first
        for k in range(slots):
            y = plane * slots + k
            value = flat[pl.ds(y, channels, stride=height), :]
            feat[y] = value.astype(jnp.bfloat16)
            if k:
                value = pltpu.roll(value, STRIP * k, 1)
            first = jnp.where(slot == k, value, first)
            last = jnp.where(slot == (k - 1) % slots, value, last)
        packed[0, plane] = first.astype(jnp.bfloat16)
        packed[1, plane] = last.astype(jnp.bfloat16)

    pl.semaphore_wait(barrier, expected)

    def copy(index, source, target, device):
        return pltpu.make_async_remote_copy(
            src_ref=source,
            dst_ref=target,
            send_sem=send_sem.at[index],
            recv_sem=recv_sem.at[index],
            device_id=device,
            device_id_type=MESH,
        )

    partner = (1 - pair, row, col)
    low = pl.ds(0, columns)
    top = pl.multiple_of(pair * half, half)
    top_there = pl.multiple_of((1 - pair) * half, half)
    body = half + 2
    piece = body // CHUNKS
    to_partner = [
        copy(
            12 + n if n else 0,
            feat.at[pl.ds((1 - pair) * (height - body) + n * piece, piece)],
            other.at[pl.ds(2 * pair + n * piece, piece), :, low],
            partner,
        )
        for n in range(CHUNKS)
    ]
    near = []
    for n, (dr, dc) in enumerate(STRIPS):
        near.append(
            (
                copy(
                    3 + n,
                    packed.at[0 if dc < 0 else 1],
                    strips.at[n],
                    (pair, row + dr, col + dc),
                ),
                (dr, dc),
                strips.at[n],
            )
        )
    for index, dr, source, target in (
        (1, 1, pl.ds(height - MARGIN, MARGIN), pl.ds(0, MARGIN)),
        (2, -1, pl.ds(0, MARGIN), pl.ds(height + MARGIN, MARGIN)),
    ):
        place = own.at[target, :, low]
        near.append((copy(index, feat.at[source], place, (pair, row + dr, col)), (dr, 0), place))

    for moved, (dr, dc), _ in near:
        pl.when(exists(dr, dc))(moved.start)
    for moved in to_partner:
        moved.start()
    for _, (dr, dc), place in near:

        @pl.when(jnp.logical_not(exists(-dr, -dc)))
        def _():
            place[...] = jnp.zeros(place.shape, place.dtype)

    own[pl.ds(MARGIN, height), :, low] = feat[...]

    for load in loads[1:]:
        load.wait()
    taps = 3 * channels
    w_self, w_cross, w_two = (
        jnp.concatenate([ref[pl.ds(taps * a, taps), pl.ds(at, channels)] for a in range(3)], axis=1)
        for ref, at in ((w_first, 0), (w_first, channels), (w_second, 0))
    )
    w_own = jnp.concatenate([w_self, w_cross], axis=0)
    w_other = jnp.concatenate([w_cross, w_self], axis=0)

    for moved, (dr, dc), _ in near:
        pl.when(exists(-dr, -dc))(moved.wait_recv)

    passed = [
        copy(9, package.at[0], package.at[1], partner),
        copy(
            10,
            own.at[pl.ds(MARGIN - 2 + (1 - pair) * (height + 2), 2), :, low],
            other.at[pl.ds((1 - pair) * body, 2), :, low],
            partner,
        ),
    ]
    passed[1].start()

    bundle = jnp.zeros((channels, columns), jnp.float32)
    needed = range(MARGIN - 2, MARGIN + height + 2)

    def unpack(i):
        side = -1 if i < MARGIN else (0 if i < MARGIN + height else 1)
        k = i - MARGIN - side * height
        left = strips[STRIPS.index((-side, 1)), k // slots].astype(jnp.float32)
        right = strips[STRIPS.index((-side, -1)), k // slots].astype(jnp.float32)
        k = k % slots
        value = jnp.where(
            slot == k, right, jnp.where(slot == (k - 1) % slots, left, 0.0)
        )
        if k:
            value = pltpu.roll(value, columns - STRIP * k, 1)
        own[i, :, pl.ds(columns, columns)] = value.astype(jnp.bfloat16)
        return value

    for j, i in enumerate(needed):
        bundle = jnp.where(lane // 4 == j, pltpu.roll(unpack(i), 2 + 4 * j, 1), bundle)
    package[0] = bundle.astype(jnp.bfloat16)

    passed[0].start()
    for i in range(height + 2 * MARGIN):
        if i not in needed:
            unpack(i)
    wide = 2 * columns

    def own_part(step, carry):
        for part in range(5):
            y = step * 5 + part
            window = own[pl.ds(top + y + MARGIN - 2, 3)].reshape(taps, wide)
            partial[y] = jnp.dot(w_own, window, preferred_element_type=jnp.float32)
        return carry

    lax.fori_loop(0, (half + 2) // 5, own_part, 0)

    passed[0].wait_recv()
    bundle = package[1].astype(jnp.float32)
    bundle = jnp.where(pair == 0, bundle, pltpu.roll(bundle, columns - 4 * half, 1))
    for j in range(half + 4):
        other[j, :, pl.ds(columns, columns)] = pltpu.roll(
            bundle, (2 * columns - 2 - 4 * j) % columns, 1
        ).astype(jnp.bfloat16)

    def joined_taps(z):
        return (
            pltpu.roll(z[:channels], 1, 1)
            + z[channels : 2 * channels]
            + pltpu.roll(z[2 * channels :], wide - 1, 1)
        )

    wide_lane = lanes((channels, wide))
    place_col = jnp.where(wide_lane < wide * 3 // 4, wide_lane, wide_lane - wide) + col * columns
    col_ok = jnp.logical_and(place_col >= 0, place_col < n_col * columns)

    def first_layer(y):
        window = other[pl.ds(y, 3)].reshape(taps, wide)
        both = partial[y] + jnp.dot(w_other, window, preferred_element_type=jnp.float32)
        if y == 0:
            ok = jnp.logical_and(col_ok, row * height + top > 0)
        elif y == half + 1:
            ok = jnp.logical_and(col_ok, row * height + top + half < n_row * height)
        else:
            ok = col_ok
        for section in range(2):
            value = joined_taps(both[section * taps : (section + 1) * taps])
            hidden[section, y] = jnp.where(ok, jnp.maximum(value, 0.0), 0.0).astype(jnp.bfloat16)

    passed[1].wait_recv()
    to_partner[0].wait_recv()
    for y in range(piece - 2):
        first_layer(y)
    for moved in to_partner[1:]:
        moved.wait_recv()
    for y in range(piece - 2, half + 2):
        first_layer(y)

    back = copy(11, residual.at[1], residual.at[2], partner)
    for section in (1, 0):
        for y in range(half):
            window = hidden[section, pl.ds(y, 3)].reshape(taps, wide)
            value = joined_taps(jnp.dot(w_two, window, preferred_element_type=jnp.float32))
            hidden_two[:, pl.ds(y * columns, columns)] = jnp.maximum(
                value[:, :columns], 0.0
            ).astype(jnp.bfloat16)
        value = jnp.tanh(jnp.dot(head[...], hidden_two[...], preferred_element_type=jnp.float32))
        for y in range(half):
            for k in range(2):
                residual[section, k, pl.ds(y, 1), :] = value[
                    k : k + 1, y * columns : (y + 1) * columns
                ]
        if section:
            back.start()

    cells = columns // BLK
    spread = (
        lax.broadcasted_iota(jnp.int32, (cells, columns), 1) // BLK
        == lax.broadcasted_iota(jnp.int32, (cells, columns), 0)
    ).astype(jnp.bfloat16)
    coverage = jnp.dot(
        tissue[...].astype(jnp.float32).astype(jnp.bfloat16),
        spread,
        preferred_element_type=jnp.float32,
    )

    def move(start, place, upper):
        cover = [
            jnp.broadcast_to(
                jnp.where(
                    upper, coverage[n : n + 1], coverage[half // BLK + n : half // BLK + n + 1]
                ),
                (BLK, columns),
            )
            for n in range(half // BLK)
        ]
        cover = jnp.concatenate(cover, axis=0) if len(cover) > 1 else cover[0]
        rows = pl.ds(start, half)
        for k in range(2):
            motion_out[k, rows, :] = (
                offsets[k, rows, :].astype(jnp.float32)
                + fractions[k, rows, :].astype(jnp.float32) / FRAC_SCALE
                + cover * residual[place, k]
            )

    depth = 2 * MARGIN + 2
    source = lax.broadcasted_iota(jnp.int32, (wide, wide), 0)
    source = jnp.where(source < wide * 3 // 4, source, source - wide).astype(jnp.float32)
    target = lanes((1, wide))
    target_col = (target % columns).astype(jnp.float32)
    target_row = (target // columns).astype(jnp.float32)
    reach = lax.broadcasted_iota(jnp.int32, (depth, wide), 0).astype(jnp.float32) - MARGIN

    def warp(y):
        both = [
            jnp.concatenate(
                [motion_out[k, pl.ds(y, 1), :], motion_out[k, pl.ds(y + 1, 1), :]], axis=1
            )
            for k in range(2)
        ]
        col_weight = jnp.maximum(1.0 - jnp.abs(both[1] + target_col - source), 0.0)
        row_weight = jnp.maximum(1.0 - jnp.abs(both[0] + target_row - reach), 0.0)
        rows = own[pl.ds(y, depth)].reshape(depth * channels, wide)
        picked = jnp.dot(
            rows, col_weight.astype(jnp.bfloat16), preferred_element_type=jnp.float32
        )
        total = None
        for d in range(depth):
            term = picked[d * channels : (d + 1) * channels] * row_weight[d : d + 1]
            total = term if total is None else total + term
        flat[pl.ds(y, channels, stride=height), :] = total[:, :columns]
        flat[pl.ds(y + 1, channels, stride=height), :] = total[:, columns:]

    for start, place, upper in ((top, 0, pair == 0), (top_there, 2, pair != 0)):
        if place:
            back.wait_recv()
        move(start, place, upper)
        for t in range(half // 2):
            warp(start + 2 * t)
    out[...] = flat[...].reshape(channels, height, columns).astype(jnp.bfloat16)

    for moved, (dr, dc), _ in near:
        pl.when(exists(dr, dc))(moved.wait_send)
    for moved in to_partner + passed + [back]:
        moved.wait_send()


def shards(n_row, n_col, features, offsets, fractions, tissue, w_first, w_second, head_weight):
    _, channels, height, columns = features.shape
    wide = 2 * columns
    vmem = pl.BlockSpec(memory_space=pltpu.VMEM)
    warped, motion = pl.pallas_call(
        functools.partial(kernel, n_row, n_col),
        out_shape=(
            pltpu.VMEM((channels, height, columns), jnp.bfloat16),
            pltpu.VMEM((2, height, columns), jnp.float32),
        ),
        in_specs=[pl.BlockSpec(memory_space=pltpu.HBM)] * 5 + [vmem] * 2,
        out_specs=(vmem, vmem),
        scratch_shapes=[
            pltpu.VMEM((height + 2 * MARGIN, channels, wide), jnp.bfloat16),
            pltpu.VMEM((height // 2 + 4, channels, wide), jnp.bfloat16),
            pltpu.VMEM((2, 2, channels, columns), jnp.bfloat16),
            pltpu.VMEM((6, 2, channels, columns), jnp.bfloat16),
            pltpu.VMEM((2, channels, columns), jnp.bfloat16),
            pltpu.VMEM((2, height // 2 + 2, channels, wide), jnp.bfloat16),
            pltpu.VMEM((channels, height // 2 * columns), jnp.bfloat16),
            pltpu.VMEM((height // 2 + 2, 6 * channels, wide), jnp.float32),
            pltpu.VMEM((3, 2, height // 2, columns), jnp.float32),
            pltpu.VMEM((channels * height, columns), jnp.float32),
            pltpu.VMEM((height, channels, columns), jnp.bfloat16),
            pltpu.VMEM((channels, height, columns), jnp.bfloat16),
            pltpu.VMEM((2, height, columns), jnp.int32),
            pltpu.VMEM((2, height, columns), jnp.int32),
            pltpu.VMEM((9 * channels, 2 * channels), jnp.bfloat16),
            pltpu.VMEM((9 * channels, channels), jnp.bfloat16),
            pltpu.SemaphoreType.DMA((N_COPIES,)),
            pltpu.SemaphoreType.DMA((N_COPIES,)),
            pltpu.SemaphoreType.DMA((5,)),
        ],
        compiler_params=pltpu.CompilerParams(
            collective_id=0, has_side_effects=True, vmem_limit_bytes=63 * 1024 * 1024
        ),
        cost_estimate=pl.CostEstimate(
            flops=4 * 10**9, bytes_accessed=2 * 10**6, transcendentals=4096
        ),
    )(
        features[0],
        offsets[0],
        fractions[0],
        w_first.reshape(-1, w_first.shape[-1]),
        w_second.reshape(-1, w_second.shape[-1]),
        tissue[0],
        head_weight,
    )
    return (warped[None], motion[None])


def solution(mesh):
    tile = P("pair", None, "row", "col")
    return jax.shard_map(
        functools.partial(shards, mesh.shape["row"], mesh.shape["col"]),
        mesh=mesh,
        in_specs=(tile, tile, tile, P("pair", "row", "col"), P(), P(), P()),
        out_specs=(tile, tile),
        check_vma=False,
    )
```

```python
import functools

import jax
import jax.numpy as jnp
from jax import lax
from jax.experimental import pallas as pl
from jax.experimental.pallas import tpu as pltpu
from jax.sharding import PartitionSpec as P

MAXS = 8
BLK = 8
MARGIN = MAXS + 1
FRAC_SCALE = 256.0
STRIP = 16
MESH = pl.DeviceIdType.MESH

STRIPS = [(dr, dc) for dr in (-1, 0, 1) for dc in (-1, 1)]
N_COPIES = 14
CHUNKS = 2


def lanes(shape):
    return lax.broadcasted_iota(jnp.int32, shape, len(shape) - 1)


def kernel(
    n_row,
    n_col,
    feat_in,
    offsets_in,
    fractions_in,
    w_first_in,
    w_second_in,
    tissue,
    head,
    out,
    motion_out,
    own,
    other,
    packed,
    strips,
    package,
    hidden,
    hidden_two,
    partial,
    residual,
    flat,
    feat,
    feat_here,
    offsets,
    fractions,
    w_first,
    w_second,
    send_sem,
    recv_sem,
    load_sem,
):
    height, channels, columns = feat.shape
    half = height // 2
    loads = [
        pltpu.make_async_copy(source, target, load_sem.at[n])
        for n, (source, target) in enumerate(
            (
                (feat_in, feat_here),
                (w_first_in, w_first),
                (w_second_in, w_second),
                (offsets_in, offsets),
                (fractions_in, fractions),
            )
        )
    ]
    for load in loads:
        load.start()
    slots = columns // STRIP
    pair = lax.axis_index("pair")
    row = lax.axis_index("row")
    col = lax.axis_index("col")

    def exists(dr, dc):
        ok = None
        for test in (
            [row + dr >= 0, row + dr < n_row] if dr else []
        ) + ([col + dc >= 0, col + dc < n_col] if dc else []):
            ok = test if ok is None else jnp.logical_and(ok, test)
        return ok

    neighbours = [(dr, dc) for dr in (-1, 0, 1) for dc in (-1, 0, 1) if dr or dc]
    barrier = pltpu.get_barrier_semaphore()
    pl.semaphore_signal(
        barrier, inc=1, device_id=(1 - pair, row, col), device_id_type=MESH
    )
    expected = jnp.int32(1)
    for dr, dc in neighbours:
        here = exists(dr, dc)
        expected = expected + here.astype(jnp.int32)

        @pl.when(here)
        def _():
            pl.semaphore_signal(
                barrier, inc=1, device_id=(pair, row + dr, col + dc), device_id_type=MESH
            )

    loads[0].wait()
    flat[...] = feat_here[...].astype(jnp.float32).reshape(channels * height, columns)

    lane = lanes((channels, columns))
    slot = lane // STRIP
    for plane in range(height // slots):
        first = jnp.zeros((channels, columns), jnp.float32)
        last = first
        for k in range(slots):
            y = plane * slots + k
            value = flat[pl.ds(y, channels, stride=height), :]
            feat[y] = value.astype(jnp.bfloat16)
            if k:
                value = pltpu.roll(value, STRIP * k, 1)
            first = jnp.where(slot == k, value, first)
            last = jnp.where(slot == (k - 1) % slots, value, last)
        packed[0, plane] = first.astype(jnp.bfloat16)
        packed[1, plane] = last.astype(jnp.bfloat16)

    pl.semaphore_wait(barrier, expected)

    def copy(index, source, target, device):
        return pltpu.make_async_remote_copy(
            src_ref=source,
            dst_ref=target,
            send_sem=send_sem.at[index],
            recv_sem=recv_sem.at[index],
            device_id=device,
            device_id_type=MESH,
        )

    partner = (1 - pair, row, col)
    low = pl.ds(0, columns)
    top = pl.multiple_of(pair * half, half)
    top_there = pl.multiple_of((1 - pair) * half, half)
    body = half + 2
    piece = body // CHUNKS
    to_partner = [
        copy(
            12 + n if n else 0,
            feat.at[pl.ds((1 - pair) * (height - body) + n * piece, piece)],
            other.at[pl.ds(2 * pair + n * piece, piece), :, low],
            partner,
        )
        for n in range(CHUNKS)
    ]
    near = []
    for n, (dr, dc) in enumerate(STRIPS):
        near.append(
            (
                copy(
                    3 + n,
                    packed.at[0 if dc < 0 else 1],
                    strips.at[n],
                    (pair, row + dr, col + dc),
                ),
                (dr, dc),
                strips.at[n],
            )
        )
    for index, dr, source, target in (
        (1, 1, pl.ds(height - MARGIN, MARGIN), pl.ds(0, MARGIN)),
        (2, -1, pl.ds(0, MARGIN), pl.ds(height + MARGIN, MARGIN)),
    ):
        place = own.at[target, :, low]
        near.append((copy(index, feat.at[source], place, (pair, row + dr, col)), (dr, 0), place))

    for moved in to_partner:
        moved.start()
    for moved, (dr, dc), _ in near:
        pl.when(exists(dr, dc))(moved.start)
    for _, (dr, dc), place in near:

        @pl.when(jnp.logical_not(exists(-dr, -dc)))
        def _():
            place[...] = jnp.zeros(place.shape, place.dtype)

    own[pl.ds(MARGIN, height), :, low] = feat[...]

    for load in loads[1:]:
        load.wait()
    taps = 3 * channels
    w_self, w_cross, w_two = (
        jnp.concatenate([ref[pl.ds(taps * a, taps), pl.ds(at, channels)] for a in range(3)], axis=1)
        for ref, at in ((w_first, 0), (w_first, channels), (w_second, 0))
    )
    w_own = jnp.concatenate([w_self, w_cross], axis=0)
    w_other = jnp.concatenate([w_cross, w_self], axis=0)

    for moved, (dr, dc), _ in near:
        pl.when(exists(-dr, -dc))(moved.wait_recv)

    passed = [
        copy(9, package.at[0], package.at[1], partner),
        copy(
            10,
            own.at[pl.ds(MARGIN - 2 + (1 - pair) * (height + 2), 2), :, low],
            other.at[pl.ds((1 - pair) * body, 2), :, low],
            partner,
        ),
    ]
    passed[1].start()

    bundle = jnp.zeros((channels, columns), jnp.float32)
    needed = range(MARGIN - 2, MARGIN + height + 2)

    def unpack(i):
        side = -1 if i < MARGIN else (0 if i < MARGIN + height else 1)
        k = i - MARGIN - side * height
        left = strips[STRIPS.index((-side, 1)), k // slots].astype(jnp.float32)
        right = strips[STRIPS.index((-side, -1)), k // slots].astype(jnp.float32)
        k = k % slots
        value = jnp.where(
            slot == k, right, jnp.where(slot == (k - 1) % slots, left, 0.0)
        )
        if k:
            value = pltpu.roll(value, columns - STRIP * k, 1)
        own[i, :, pl.ds(columns, columns)] = value.astype(jnp.bfloat16)
        return value

    for j, i in enumerate(needed):
        bundle = jnp.where(lane // 4 == j, pltpu.roll(unpack(i), 2 + 4 * j, 1), bundle)
    package[0] = bundle.astype(jnp.bfloat16)

    passed[0].start()
    for i in range(height + 2 * MARGIN):
        if i not in needed:
            unpack(i)
    wide = 2 * columns

    def own_part(step, carry):
        for part in range(5):
            y = step * 5 + part
            window = own[pl.ds(top + y + MARGIN - 2, 3)].reshape(taps, wide)
            partial[y] = jnp.dot(w_own, window, preferred_element_type=jnp.float32)
        return carry

    lax.fori_loop(0, (half + 2) // 5, own_part, 0)

    passed[0].wait_recv()
    bundle = package[1].astype(jnp.float32)
    bundle = jnp.where(pair == 0, bundle, pltpu.roll(bundle, columns - 4 * half, 1))
    for j in range(half + 4):
        other[j, :, pl.ds(columns, columns)] = pltpu.roll(
            bundle, (2 * columns - 2 - 4 * j) % columns, 1
        ).astype(jnp.bfloat16)

    def joined_taps(z):
        return (
            pltpu.roll(z[:channels], 1, 1)
            + z[channels : 2 * channels]
            + pltpu.roll(z[2 * channels :], wide - 1, 1)
        )

    wide_lane = lanes((channels, wide))
    place_col = jnp.where(wide_lane < wide * 3 // 4, wide_lane, wide_lane - wide) + col * columns
    col_ok = jnp.logical_and(place_col >= 0, place_col < n_col * columns)

    def first_layer(y):
        window = other[pl.ds(y, 3)].reshape(taps, wide)
        both = partial[y] + jnp.dot(w_other, window, preferred_element_type=jnp.float32)
        if y == 0:
            ok = jnp.logical_and(col_ok, row * height + top > 0)
        elif y == half + 1:
            ok = jnp.logical_and(col_ok, row * height + top + half < n_row * height)
        else:
            ok = col_ok
        for section in range(2):
            value = joined_taps(both[section * taps : (section + 1) * taps])
            hidden[section, y] = jnp.where(ok, jnp.maximum(value, 0.0), 0.0).astype(jnp.bfloat16)

    passed[1].wait_recv()
    to_partner[0].wait_recv()
    for y in range(piece - 2):
        first_layer(y)
    for moved in to_partner[1:]:
        moved.wait_recv()
    for y in range(piece - 2, half + 2):
        first_layer(y)

    back = copy(11, residual.at[1], residual.at[2], partner)
    for section in (1, 0):
        for y in range(half):
            window = hidden[section, pl.ds(y, 3)].reshape(taps, wide)
            value = joined_taps(jnp.dot(w_two, window, preferred_element_type=jnp.float32))
            hidden_two[:, pl.ds(y * columns, columns)] = jnp.maximum(
                value[:, :columns], 0.0
            ).astype(jnp.bfloat16)
        value = jnp.tanh(jnp.dot(head[...], hidden_two[...], preferred_element_type=jnp.float32))
        for y in range(half):
            for k in range(2):
                residual[section, k, pl.ds(y, 1), :] = value[
                    k : k + 1, y * columns : (y + 1) * columns
                ]
        if section:
            back.start()

    cells = columns // BLK
    spread = (
        lax.broadcasted_iota(jnp.int32, (cells, columns), 1) // BLK
        == lax.broadcasted_iota(jnp.int32, (cells, columns), 0)
    ).astype(jnp.bfloat16)
    coverage = jnp.dot(
        tissue[...].astype(jnp.float32).astype(jnp.bfloat16),
        spread,
        preferred_element_type=jnp.float32,
    )

    def move(start, place, upper):
        cover = [
            jnp.broadcast_to(
                jnp.where(
                    upper, coverage[n : n + 1], coverage[half // BLK + n : half // BLK + n + 1]
                ),
                (BLK, columns),
            )
            for n in range(half // BLK)
        ]
        cover = jnp.concatenate(cover, axis=0) if len(cover) > 1 else cover[0]
        rows = pl.ds(start, half)
        for k in range(2):
            motion_out[k, rows, :] = (
                offsets[k, rows, :].astype(jnp.float32)
                + fractions[k, rows, :].astype(jnp.float32) / FRAC_SCALE
                + cover * residual[place, k]
            )

    depth = 2 * MARGIN + 2
    source = lax.broadcasted_iota(jnp.int32, (wide, wide), 0)
    source = jnp.where(source < wide * 3 // 4, source, source - wide).astype(jnp.float32)
    target = lanes((1, wide))
    target_col = (target % columns).astype(jnp.float32)
    target_row = (target // columns).astype(jnp.float32)
    reach = lax.broadcasted_iota(jnp.int32, (depth, wide), 0).astype(jnp.float32) - MARGIN

    def warp(y):
        both = [
            jnp.concatenate(
                [motion_out[k, pl.ds(y, 1), :], motion_out[k, pl.ds(y + 1, 1), :]], axis=1
            )
            for k in range(2)
        ]
        col_weight = jnp.maximum(1.0 - jnp.abs(both[1] + target_col - source), 0.0)
        row_weight = jnp.maximum(1.0 - jnp.abs(both[0] + target_row - reach), 0.0)
        rows = own[pl.ds(y, depth)].reshape(depth * channels, wide)
        picked = jnp.dot(
            rows, col_weight.astype(jnp.bfloat16), preferred_element_type=jnp.float32
        )
        total = None
        for d in range(depth):
            term = picked[d * channels : (d + 1) * channels] * row_weight[d : d + 1]
            total = term if total is None else total + term
        flat[pl.ds(y, channels, stride=height), :] = total[:, :columns]
        flat[pl.ds(y + 1, channels, stride=height), :] = total[:, columns:]

    for start, place, upper in ((top, 0, pair == 0), (top_there, 2, pair != 0)):
        if place:
            back.wait_recv()
        move(start, place, upper)
        for t in range(half // 2):
            warp(start + 2 * t)
    out[...] = flat[...].reshape(channels, height, columns).astype(jnp.bfloat16)

    for moved, (dr, dc), _ in near:
        pl.when(exists(dr, dc))(moved.wait_send)
    for moved in to_partner + passed + [back]:
        moved.wait_send()


def shards(n_row, n_col, features, offsets, fractions, tissue, w_first, w_second, head_weight):
    _, channels, height, columns = features.shape
    wide = 2 * columns
    vmem = pl.BlockSpec(memory_space=pltpu.VMEM)
    warped, motion = pl.pallas_call(
        functools.partial(kernel, n_row, n_col),
        out_shape=(
            pltpu.VMEM((channels, height, columns), jnp.bfloat16),
            pltpu.VMEM((2, height, columns), jnp.float32),
        ),
        in_specs=[pl.BlockSpec(memory_space=pltpu.HBM)] * 5 + [vmem] * 2,
        out_specs=(vmem, vmem),
        scratch_shapes=[
            pltpu.VMEM((height + 2 * MARGIN, channels, wide), jnp.bfloat16),
            pltpu.VMEM((height // 2 + 4, channels, wide), jnp.bfloat16),
            pltpu.VMEM((2, 2, channels, columns), jnp.bfloat16),
            pltpu.VMEM((6, 2, channels, columns), jnp.bfloat16),
            pltpu.VMEM((2, channels, columns), jnp.bfloat16),
            pltpu.VMEM((2, height // 2 + 2, channels, wide), jnp.bfloat16),
            pltpu.VMEM((channels, height // 2 * columns), jnp.bfloat16),
            pltpu.VMEM((height // 2 + 2, 6 * channels, wide), jnp.float32),
            pltpu.VMEM((3, 2, height // 2, columns), jnp.float32),
            pltpu.VMEM((channels * height, columns), jnp.float32),
            pltpu.VMEM((height, channels, columns), jnp.bfloat16),
            pltpu.VMEM((channels, height, columns), jnp.bfloat16),
            pltpu.VMEM((2, height, columns), jnp.int32),
            pltpu.VMEM((2, height, columns), jnp.int32),
            pltpu.VMEM((9 * channels, 2 * channels), jnp.bfloat16),
            pltpu.VMEM((9 * channels, channels), jnp.bfloat16),
            pltpu.SemaphoreType.DMA((N_COPIES,)),
            pltpu.SemaphoreType.DMA((N_COPIES,)),
            pltpu.SemaphoreType.DMA((5,)),
        ],
        compiler_params=pltpu.CompilerParams(
            collective_id=0, has_side_effects=True, vmem_limit_bytes=63 * 1024 * 1024
        ),
        cost_estimate=pl.CostEstimate(
            flops=4 * 10**9, bytes_accessed=2 * 10**6, transcendentals=4096
        ),
    )(
        features[0],
        offsets[0],
        fractions[0],
        w_first.reshape(-1, w_first.shape[-1]),
        w_second.reshape(-1, w_second.shape[-1]),
        tissue[0],
        head_weight,
    )
    return (warped[None], motion[None])


def solution(mesh):
    tile = P("pair", None, "row", "col")
    return jax.shard_map(
        functools.partial(shards, mesh.shape["row"], mesh.shape["col"]),
        mesh=mesh,
        in_specs=(tile, tile, tile, P("pair", "row", "col"), P(), P(), P()),
        out_specs=(tile, tile),
        check_vma=False,
    )
```
